32 devices in a mesh: parts: 2 (over y), brick: 4 (over z), case: 4 (over x, core).
Axes of the slice: x: 2, y: 2, z: 4, core: 2. Of those that a mesh axis runs over, the one named last changes fastest.
Arguments:
- density: float32 [16, 64, 128], P(('parts', 'brick')), parts along dimension 0, may hold values from 0.3 to 1
- phase: int32 [16, 64, 128], P(('parts', 'brick')), parts along dimension 0, may hold values from 0 to 2
- warm_start: float32 [16, 3, 8, 64, 128], P(('parts', 'case'), None, 'brick'), parts along dimension 0, may hold values from -1.2 to 1.2
- case_table: int32 [8], replicated, may hold values from 0 to 7, each once
- multiplier: float32 [8, 8], replicated, may hold values from -1.5 to 1.5
- target: float32 [8, 8], replicated, may hold values from 0 to 0.4
- penalty_steps: int32 [8, 8], replicated, may hold values from 0 to 3
Outputs:
- fluctuation: float32 [16, 3, 8, 64, 128], P(('parts', 'case'), None, 'brick'), parts along dimension 0
- tensor: float32 [16, 8], P(('parts', 'case')), parts along dimension 0
- design_gradient: float32 [16, 64, 128], P(('parts', 'brick'), 'case'), parts along dimension 0
The draws below stay inside these ranges and needn't reach their ends.
There are 2 independent parts, one for each index of `parts`. The reference program is written for one: setup_inputs(seed, part) draws one part's arguments, and reference() takes and returns one part's arrays. A program takes and returns all parts, laid end to end along the dimension named above; an argument that names none is the same for every part. Nothing has to cross between parts.
Inputs may be any that keep to these rules, and one draw needn't show every extreme that they name: `case_table`: a permutation of 0 to 7: values 0 to 5 name the six unit strains once each, larger values mark padded cases.
All inputs are finite; a program needn't handle non-finite values.
Results may differ from the reference program's by a relative error of at most 0.0002.
Values sent between devices are 32-bit elements; how exact they have to be, the bound alone decides.
A program may use at most 64 MiB of HBM per device.

```python
import jax
import jax.numpy as jnp
import numpy as np
from jax import lax

NY = 64
NZ = 128
ITERS = 2
CASES = 8
NX = 8


def place_ends(drawn, stream_key, low, largest):
    spot = [jax.random.randint(jax.random.fold_in(stream_key, axis), (), 0, length) for axis, length in enumerate(drawn.shape)]
    longest = drawn.shape.index(max(drawn.shape))
    neighbour = spot[:longest] + [(spot[longest] + 1) % drawn.shape[longest]] + spot[longest + 1:]
    return drawn.at[tuple(spot)].set(low).at[tuple(neighbour)].set(largest)


def block_scale(own_key, dims, pieces, smallest, top_value):
    loudness = 1.0
    for axis_at, shards_of in pieces:
        heights = jax.random.uniform(jax.random.fold_in(jax.random.fold_in(own_key, 6), axis_at), (shards_of,), jnp.float32, smallest / len(pieces), top_value / len(pieces))
        loudness = loudness * jnp.repeat(jnp.exp(heights), dims[axis_at] // shards_of).reshape((-1,) + (1,) * (len(dims) - 1 - axis_at))
    return loudness


def scatter_about(stream_key, extent, deviation, limit, shards=(), kind=jnp.bfloat16):
    drawn = deviation * jax.random.normal(stream_key, extent, jnp.float32)
    if shards:
        drawn = drawn * block_scale(stream_key, extent, shards, -0.22, 0.18)
    return jnp.clip(drawn, -limit, limit).astype(kind)


def setup_inputs(seed: int = 0, part: int = 0) -> dict:
    key_list = jax.random.split(jax.random.key(seed), 8)
    part_splits = jax.random.split(jax.random.fold_in(key_list[7], part), 8)
    density = jnp.clip(0.3 + 0.7 * jax.random.uniform(part_splits[0], (NX, NY, NZ), jnp.float32) ** block_scale(part_splits[0], (NX, NY, NZ), ((0, 4),), -0.2, 0.2), 0.3, 1.0)
    phase = place_ends(jax.random.randint(part_splits[1], (NX, NY, NZ), 0, 3), jax.random.fold_in(part_splits[1], 1), 0, 2).astype(jnp.int32)
    warm_start = scatter_about(part_splits[2], (CASES, 3, NX, NY, NZ), 0.2, 1.2, ((0, 4), (2, 4)), jnp.float32)
    case_table = jax.random.permutation(key_list[3], CASES).astype(jnp.int32)
    multiplier = scatter_about(key_list[4], (CASES, CASES), 0.3, 1.5, (), jnp.float32)
    target = jnp.clip(jax.random.uniform(key_list[5], (CASES, CASES), jnp.float32, 0.0, 0.4), 0.0, 0.4)
    penalty_steps = place_ends(jax.random.randint(key_list[6], (CASES, CASES), 0, 4), jax.random.fold_in(key_list[6], 1), 0, 3).astype(jnp.int32)
    return dict(density=density, phase=phase, warm_start=warm_start, case_table=case_table, multiplier=multiplier, target=target, penalty_steps=penalty_steps)


def element_matrix():
    ratio = 0.3
    lame = ratio / ((1.0 + ratio) * (1.0 - 2.0 * ratio))
    shear = 1.0 / (2.0 * (1.0 + ratio))
    elastic = np.zeros((6, 6))
    elastic[:3, :3] = lame
    for index in range(3):
        elastic[index, index] = lame + 2.0 * shear
        elastic[index + 3, index + 3] = shear
    points = [0.5 - 0.5 / np.sqrt(3.0), 0.5 + 0.5 / np.sqrt(3.0)]
    result = np.zeros((24, 24))
    for gx in points:
        for gy in points:
            for gz in points:
                strain_map = np.zeros((6, 24))
                for a in range(2):
                    for b in range(2):
                        for c in range(2):
                            node = 4 * a + 2 * b + c
                            fx = gx if a else 1.0 - gx
                            fy = gy if b else 1.0 - gy
                            fz = gz if c else 1.0 - gz
                            sx = 1.0 if a else -1.0
                            sy = 1.0 if b else -1.0
                            sz = 1.0 if c else -1.0
                            dxn = sx * fy * fz
                            dyn = fx * sy * fz
                            dzn = fx * fy * sz
                            strain_map[0, node] = dxn
                            strain_map[1, 8 + node] = dyn
                            strain_map[2, 16 + node] = dzn
                            strain_map[3, 8 + node] = dzn
                            strain_map[3, 16 + node] = dyn
                            strain_map[4, node] = dzn
                            strain_map[4, 16 + node] = dxn
                            strain_map[5, node] = dyn
                            strain_map[5, 8 + node] = dxn
                result = result + strain_map.T @ elastic @ strain_map / 8.0
    return result

def strain_table():
    table = np.zeros((6, 24))
    for a in range(2):
        for b in range(2):
            for c in range(2):
                node = 4 * a + 2 * b + c
                table[0, node] = a
                table[1, 8 + node] = b
                table[2, 16 + node] = c
                table[3, 8 + node] = 0.5 * c
                table[3, 16 + node] = 0.5 * b
                table[4, node] = 0.5 * c
                table[4, 16 + node] = 0.5 * a
                table[5, node] = 0.5 * b
                table[5, 8 + node] = 0.5 * a
    return table
corner_list = [(comp, a, b, c) for comp in range(3) for a in range(2) for b in range(2) for c in range(2)]

def corners(field):
    return jnp.stack([jnp.roll(field[comp], (-a, -b, -c), axis=(0, 1, 2)) for comp, a, b, c in corner_list])

def spread(forces):
    result = []
    for comp in range(3):
        total = jnp.zeros(forces.shape[1:], forces.dtype)
        for a in range(2):
            for b in range(2):
                for c in range(2):
                    total = total + jnp.roll(forces[comp * 8 + 4 * a + 2 * b + c], (a, b, c), axis=(0, 1, 2))
        result.append(total)
    return jnp.stack(result)

def reference(density, phase, warm_start, case_table, multiplier, target, penalty_steps):
    highest = lax.Precision.HIGHEST
    stiffness = jnp.asarray(element_matrix(), jnp.float32)
    table = jnp.asarray(strain_table(), jnp.float32)
    factor = 0.5 + 0.5 * (phase >= 1).astype(jnp.float32) + 1.0 * (phase >= 2).astype(jnp.float32)
    moduli = 0.05 + density ** 3 * factor
    slope = 3.0 * density ** 2 * factor
    onehot = (case_table[:, None] == jnp.arange(6, dtype=jnp.int32)[None, :]).astype(jnp.float32)
    strains = jnp.dot(onehot, table, precision=highest)
    active = (case_table < 6).astype(jnp.float32)

    def operate(field):
        forces = jnp.einsum('pq,qxyz->pxyz', stiffness, corners(field), precision=highest)
        return spread(moduli[None] * forces)

    def solve(inputs):
        start, strain = inputs
        element_load = jnp.dot(stiffness, strain, precision=highest)
        load = spread(moduli[None] * element_load[:, None, None, None])
        solution = start
        residual = load - operate(start)
        direction = residual
        norm_now = jnp.sum(residual * residual)
        for step in range(ITERS):
            image = operate(direction)
            alpha = norm_now / jnp.sum(direction * image)
            solution = solution + alpha * direction
            residual = residual - alpha * image
            norm_next = jnp.sum(residual * residual)
            direction = residual + norm_next / norm_now * direction
            norm_now = norm_next
        return solution
    fluctuation = lax.map(solve, (warm_start, strains))

    def adjoint(inputs):
        field, strain = inputs
        return strain[:, None, None, None] - corners(field)
    vectors = lax.map(adjoint, (fluctuation, strains))

    def pair_row(vector):
        loaded = jnp.einsum('pq,qxyz->pxyz', stiffness, vector, precision=highest)
        return jnp.einsum('jpxyz,pxyz->jxyz', vectors, loaded, precision=highest)
    pairs = lax.map(pair_row, vectors)
    tensor = jnp.einsum('ijxyz,xyz->ij', pairs, moduli, precision=highest) / (NX * NY * NZ)
    penalty = 0.25 * jnp.exp2(penalty_steps.astype(jnp.float32))
    weights = active[:, None] * active[None, :] * (multiplier + penalty * (tensor - target))
    design_gradient = slope * jnp.einsum('ij,ijxyz->xyz', weights, pairs, precision=highest)
    return (fluctuation, tensor, design_gradient)
```

```python
import functools

import jax
import jax.numpy as jnp
import numpy as np
from jax import lax
from jax.experimental import pallas as pl
from jax.experimental.pallas import tpu as pltpu
from jax.sharding import PartitionSpec as P


def element_matrix():
    ratio = 0.3
    lame = ratio / ((1.0 + ratio) * (1.0 - 2.0 * ratio))
    shear = 1.0 / (2.0 * (1.0 + ratio))
    elastic = np.zeros((6, 6))
    elastic[:3, :3] = lame
    for index in range(3):
        elastic[index, index] = lame + 2.0 * shear
        elastic[index + 3, index + 3] = shear
    points = [0.5 - 0.5 / np.sqrt(3.0), 0.5 + 0.5 / np.sqrt(3.0)]
    result = np.zeros((24, 24))
    for gx in points:
        for gy in points:
            for gz in points:
                strain_map = np.zeros((6, 24))
                for a in range(2):
                    for b in range(2):
                        for c in range(2):
                            node = 4 * a + 2 * b + c
                            fx = gx if a else 1.0 - gx
                            fy = gy if b else 1.0 - gy
                            fz = gz if c else 1.0 - gz
                            sx = 1.0 if a else -1.0
                            sy = 1.0 if b else -1.0
                            sz = 1.0 if c else -1.0
                            dxn = sx * fy * fz
                            dyn = fx * sy * fz
                            dzn = fx * fy * sz
                            strain_map[0, node] = dxn
                            strain_map[1, 8 + node] = dyn
                            strain_map[2, 16 + node] = dzn
                            strain_map[3, 8 + node] = dzn
                            strain_map[3, 16 + node] = dyn
                            strain_map[4, node] = dzn
                            strain_map[4, 16 + node] = dxn
                            strain_map[5, node] = dyn
                            strain_map[5, 8 + node] = dxn
                result = result + strain_map.T @ elastic @ strain_map / 8.0
    return result


def strain_table():
    table = np.zeros((6, 24))
    for a in range(2):
        for b in range(2):
            for c in range(2):
                node = 4 * a + 2 * b + c
                table[0, node] = a
                table[1, 8 + node] = b
                table[2, 16 + node] = c
                table[3, 8 + node] = 0.5 * c
                table[3, 16 + node] = 0.5 * b
                table[4, node] = 0.5 * c
                table[4, 16 + node] = 0.5 * a
                table[5, node] = 0.5 * b
                table[5, 8 + node] = 0.5 * a
    return table


def mode_factor():
    butterfly = np.array([[1.0, 1.0], [-1.0, 1.0]])
    modes = np.kron(np.eye(3), np.kron(butterfly, np.kron(butterfly, butterfly)))
    left = modes @ element_matrix() @ modes.T / 64.0
    rows = []
    for index in range(24):
        if left[index, index] > 1e-9:
            row = left[index] / np.sqrt(left[index, index])
            row[np.abs(row) < 1e-9] = 0.0
            rows.append(row)
            left = left - np.outer(row, row)
    factor = np.stack(rows)
    unit = strain_table() @ modes.T @ factor.T
    unit[np.abs(unit) < 1e-9] = 0.0
    rows = [[(int(i), float(row[i])) for i in np.nonzero(row)[0]] for row in factor]
    columns = [
        [(j, float(factor[j, i])) for j in range(len(rows)) if factor[j, i] != 0.0]
        for i in range(24)
    ]
    return rows, columns, unit


ROWS, COLUMNS, UNIT = mode_factor()
TERMS = len(ROWS)
PAIRS = [(i, j) for i in range(8) for j in range(i, 8)]


def total_of(terms):
    return functools.reduce(lambda x, y: x + y, terms)


def plane_modes(v):
    ahead = pltpu.roll(v, v.shape[1] - 1, 1)
    result = [None] * 4
    for c, part in enumerate((v + ahead, ahead - v)):
        up = pltpu.roll(part, v.shape[0] - 1, 0)
        result[c] = part + up
        result[2 + c] = up - part
    return result


def plane_spread(g):
    sums = [g[c] - g[2 + c] + pltpu.roll(g[c] + g[2 + c], 1, 0) for c in range(2)]
    return sums[0] - sums[1] + pltpu.roll(sums[0] + sums[1], 1, 1)


def cell_terms(lower, upper):
    modes = {}
    for comp in range(3):
        for bc in range(4):
            lo, hi = lower[comp * 4 + bc], upper[comp * 4 + bc]
            modes[comp * 8 + bc] = lo + hi
            modes[comp * 8 + 4 + bc] = hi - lo
    return [total_of([weight * modes[i] for i, weight in row]) for row in ROWS]


def cell_spread(terms):
    lower, upper = [], []
    for comp in range(3):
        for bc in range(4):
            even = COLUMNS[comp * 8 + bc]
            odd = COLUMNS[comp * 8 + 4 + bc]
            slope = total_of([weight * terms[j] for j, weight in odd])
            if even:
                mean = total_of([weight * terms[j] for j, weight in even])
                lower.append(mean - slope)
                upper.append(mean + slope)
            else:
                lower.append(-slope)
                upper.append(slope)
    return lower, upper


def unit_terms(name):
    result = {}
    for j in range(TERMS):
        picks = [
            jnp.where(name == s, float(UNIT[s, j]), 0.0) for s in range(6) if UNIT[s, j] != 0.0
        ]
        if picks:
            result[j] = total_of(picks)
    return result


def fold(x):
    return jnp.sum(x.reshape(-1, 8, x.shape[-1]), axis=0)


def kernel(
    bricks, groups, table, multiplier, target, steps, density, phase, warm,
    fluct, tensor, gradient,
    moduli, slope, below, above, modes, forces, res, image, packed, fields, terms,
    products, sums, spread, reduced, first, second,
    modulus_send, modulus_recv, warm_send, warm_recv, res_send, res_recv,
    red_send, red_recv, field_send, field_recv, first_send, first_recv, second_send, second_recv,
):
    brick = lax.axis_index("brick")
    group = lax.axis_index("case")
    height, width = warm.shape[3], warm.shape[4]
    slab = height // groups
    up = lax.rem(brick + 1, bricks)
    down = lax.rem(brick + bricks - 1, bricks)

    barrier = pltpu.get_barrier_semaphore()
    for step in range(1, bricks):
        pl.semaphore_signal(
            barrier, inc=1, device_id={"brick": lax.rem(brick + step, bricks)},
            device_id_type=pl.DeviceIdType.MESH,
        )
    for step in range(1, groups):
        pl.semaphore_signal(
            barrier, inc=1, device_id={"case": lax.rem(group + step, groups)},
            device_id_type=pl.DeviceIdType.MESH,
        )

    kind = phase[...]
    scale = 0.5 + 0.5 * (kind >= 1).astype(jnp.float32) + 1.0 * (kind >= 2).astype(jnp.float32)
    square = density[...] * density[...]
    moduli[1:3] = 0.05 + square * density[...] * scale
    slope[...] = 3.0 * square * scale

    pl.semaphore_wait(barrier, bricks + groups - 2)
    pending = []

    def send(src, dst, send_sem, recv_sem, **where):
        copy = pltpu.make_async_remote_copy(
            src_ref=src, dst_ref=dst, send_sem=send_sem, recv_sem=recv_sem,
            device_id=where, device_id_type=pl.DeviceIdType.MESH,
        )
        copy.start()
        pending.append(copy)
        return copy

    modulus_copies = [
        send(moduli.at[1], moduli.at[3], modulus_send.at[0], modulus_recv.at[0], brick=down),
        send(moduli.at[2], moduli.at[0], modulus_send.at[1], modulus_recv.at[1], brick=up),
    ]
    warm_copies = [
        [
            send(warm.at[k, :, 0], above.at[k], warm_send.at[k, 0], warm_recv.at[k, 0], brick=down),
            send(warm.at[k, :, 1], below.at[k], warm_send.at[k, 1], warm_recv.at[k, 1], brick=up),
        ]
        for k in range(2)
    ]

    def into_modes(k, node, values):
        for comp in range(3):
            for bc, part in enumerate(plane_modes(values(comp))):
                modes[k, node, comp * 4 + bc] = part

    def apply(k, first_element, count, constant):
        def chunk(index, carry):
            rows = pl.ds(pl.multiple_of(index * 8, 8), 8)
            lower = [modes[k, 0, i, rows] for i in range(12)]
            before = None
            for e in range(count):
                upper = [modes[k, e + 1, i, rows] for i in range(12)]
                found = cell_terms(lower, upper)
                if constant is not None:
                    found = [
                        constant[j] - z if j in constant else -z for j, z in enumerate(found)
                    ]
                modulus = moduli[e, rows]
                on_lower, on_upper = cell_spread([modulus * z for z in found])
                if before is not None:
                    for i in range(12):
                        forces[e - 1, i, rows] = before[i] + on_lower[i]
                before = on_upper
                lower = upper
            return carry

        lax.fori_loop(0, height // 8, chunk, 0)

    def node_force(node, comp):
        return plane_spread([forces[node, comp * 4 + bc] for bc in range(4)])

    for k in range(2):
        for node in range(2):
            into_modes(k, node + 1, lambda comp: warm[k, comp, node])
    res_copies = []
    for k in range(2):
        if k == 0:
            for copy in modulus_copies:
                copy.wait_recv()
        for copy in warm_copies[k]:
            copy.wait_recv()
        into_modes(k, 0, lambda comp: below[k, comp])
        into_modes(k, 3, lambda comp: above[k, comp])
        apply(k, 0, 3, unit_terms(table[group * 2 + k]))
        for node in range(2):
            for comp in range(3):
                res[k, node + 1, comp] = node_force(node, comp)
        res_copies.append([
            send(res.at[k, pl.ds(1, 2)], res.at[k, pl.ds(3, 2)], res_send.at[k, 0], res_recv.at[k, 0], brick=down),
            send(res.at[k, 2], res.at[k, 0], res_send.at[k, 1], res_recv.at[k, 1], brick=up),
        ])
    red_copies = []
    for k in range(2):
        for node in (1, 2):
            into_modes(k, node, lambda comp: res[k, node, comp])
        for copy in res_copies[k]:
            copy.wait_recv()
        for node in (0, 3, 4):
            into_modes(k, node, lambda comp: res[k, node, comp])
        apply(k, 0, 4, None)
        squares = [jnp.zeros((8, width), jnp.float32) for _ in range(3)]
        for node in range(3):
            for comp in range(3):
                value = node_force(node, comp)
                image[k, node, comp] = value
                for bc, part in enumerate(plane_modes(value)):
                    modes[k, node, comp * 4 + bc] = part
                if node < 2:
                    own = res[k, node + 1, comp]
                    squares[0] += fold(own * own)
                    squares[1] += fold(own * value)
                    squares[2] += fold(value * value)

        def energy(index, carry):
            rows = pl.ds(pl.multiple_of(index * 8, 8), 8)
            lower = [modes[k, 0, i, rows] for i in range(12)]
            for e in range(2):
                upper = [modes[k, e + 1, i, rows] for i in range(12)]
                found = cell_terms(lower, upper)
                carry = carry + moduli[e + 1, rows] * total_of([z * z for z in found])
                lower = upper
            return carry

        squares.append(lax.fori_loop(0, height // 8, energy, jnp.zeros((8, width), jnp.float32)))
        lines = [jnp.sum(s, axis=0, keepdims=True) for s in squares]
        lines.append(jnp.zeros((4, width), jnp.float32))
        reduced[k, brick] = jnp.concatenate(lines, axis=0)
        red_copies.append([
            send(
                reduced.at[k, brick], reduced.at[k, brick], red_send.at[k, step - 1],
                red_recv.at[k, step - 1], brick=lax.rem(brick + step, bricks),
            )
            for step in range(1, bricks)
        ])
    field_copies = []
    for k in range(2):
        for copy in red_copies[k]:
            copy.wait_recv()
        moments = jnp.sum(jnp.sum(reduced[k], axis=0), axis=1, keepdims=True)
        rr, rar, pp, pap = (moments[i : i + 1] for i in range(4))
        alpha = rr / rar
        later = alpha * alpha * pp - rr
        grow = 1.0 + later / rr
        curve = grow * grow * rar - 2.0 * grow * alpha * pp + alpha * alpha * pap
        alpha_later = later / curve
        on_res = alpha + alpha_later * grow
        on_image = -alpha_later * alpha
        for node in range(3):
            for comp in range(3):
                start = above[k, comp] if node == 2 else warm[k, comp, node]
                value = start + on_res * res[k, node + 1, comp] + on_image * image[k, node, comp]
                if node < 2:
                    fluct[k, comp, node] = value
                place = node * 3 + comp
                for g in range(groups):
                    packed[k, g, place * slab : (place + 1) * slab] = value[g * slab : (g + 1) * slab]
                    edge = (g + 1) * slab % height
                    packed[k, g, 9 * slab + place : 9 * slab + place + 1] = value[edge : edge + 1]
        for g in range(groups):
            packed[k, g, 9 * slab + 9 : 9 * slab + 16] = jnp.zeros((7, width), jnp.float32)
        field_copies.append([])
        for step in range(1, groups):
            peer = lax.rem(group + step, groups)
            field_copies[k].append(send(
                packed.at[k, peer], fields.at[group * 2 + k], field_send.at[k, step - 1],
                field_recv.at[k, step - 1], case=peer,
            ))
        fields[group * 2 + k] = packed[k, group]

    last = lax.broadcasted_iota(jnp.int32, (slab, width), 0) == slab - 1

    def case_terms(k, which):
        constant = unit_terms(table[which])
        lower = None
        for node in range(3):
            upper = []
            for comp in range(3):
                place = node * 3 + comp
                v = fields[which, place * slab : (place + 1) * slab]
                edge = fields[which, 9 * slab + place : 9 * slab + place + 1]
                next_v = jnp.where(last, edge, pltpu.roll(v, slab - 1, 0))
                ahead, next_ahead = pltpu.roll(v, width - 1, 1), pltpu.roll(next_v, width - 1, 1)
                s, d = v + ahead, ahead - v
                ns, nd = next_v + next_ahead, next_ahead - next_v
                upper += [s + ns, d + nd, ns - s, nd - d]
            if lower is not None:
                found = cell_terms(lower, upper)
                for j, z in enumerate(found):
                    terms[which, j, node - 1] = constant[j] - z if j in constant else -z
            lower = upper

    for k in range(2):
        case_terms(k, group * 2 + k)
    for k in range(2):
        for step in range(1, groups):
            field_copies[k][step - 1].wait_recv()
            case_terms(k, lax.rem(group + groups - step, groups) * 2 + k)

    own_rows = pl.ds(pl.multiple_of(group * slab, slab), slab)
    own_moduli = moduli[1:3, own_rows]
    for index, (i, j) in enumerate(PAIRS):
        value = terms[i, 0] * terms[j, 0]
        for t in range(1, TERMS):
            value = value + terms[i, t] * terms[j, t]
        products[index] = value
        line = jnp.sum(fold((value * own_moduli).reshape(2 * slab, width)), axis=0, keepdims=True)
        sums[i * 8 + j : i * 8 + j + 1] = line
        if i != j:
            sums[j * 8 + i : j * 8 + i + 1] = line
    totals = jnp.sum(sums[...], axis=1, keepdims=True)
    lane = lax.broadcasted_iota(jnp.int32, (8, width), 1)
    row = lax.broadcasted_iota(jnp.int32, (8, width), 0)
    tile = jnp.zeros((8, width), jnp.float32)
    for i in range(8):
        line = jnp.sum(jnp.where(lane == row, totals[i * 8 : i * 8 + 8], 0.0), axis=0, keepdims=True)
        tile = jnp.where(row == i, line, tile)
    first[group] = tile
    copies = [
        send(first.at[group], first.at[group], first_send.at[step - 1], first_recv.at[step - 1], case=lax.rem(group + step, groups))
        for step in range(1, groups)
    ]
    for copy in copies:
        copy.wait_recv()
    second[brick] = jnp.sum(first[...], axis=0)
    copies = [
        send(second.at[brick], second.at[brick], second_send.at[step - 1], second_recv.at[step - 1], brick=lax.rem(brick + step, bricks))
        for step in range(1, bricks)
    ]
    for copy in copies:
        copy.wait_recv()
    tile = jnp.sum(second[...], axis=0) * (1.0 / (bricks * 2 * height * width))
    for k in range(2):
        line = jnp.sum(jnp.where(row == group * 2 + k, tile, 0.0), axis=0, keepdims=True)
        tensor[k : k + 1] = line[:, :8]
    for i in range(8):
        picked = jnp.where(lane == row, jnp.broadcast_to(tile[i : i + 1], (8, width)), 0.0)
        spread[i * 8 : i * 8 + 8] = jnp.broadcast_to(jnp.sum(picked, axis=1, keepdims=True), (8, width))

    def weight(i, j):
        penalty = 0.25 * (jnp.int32(1) << steps[i, j]).astype(jnp.float32)
        return multiplier[i, j] + penalty * (spread[i * 8 + j : i * 8 + j + 1] - target[i, j])

    active = [jnp.where(table[i] < 6, 1.0, 0.0) for i in range(8)]
    result = jnp.zeros((2, slab, width), jnp.float32)
    for index, (i, j) in enumerate(PAIRS):
        both = weight(i, j) if i == j else weight(i, j) + weight(j, i)
        both = (active[i] * active[j]) * both
        result = result + both[None] * products[index]
    gradient[...] = slope[:, own_rows] * result
    for copy in pending:
        copy.wait_send()


def on_device(bricks, groups, density, phase, warm_start, case_table, multiplier, target, penalty_steps):
    height, width = density.shape[1:]
    slab = height // groups
    f32 = jnp.float32
    vmem = pl.BlockSpec(memory_space=pltpu.VMEM)
    smem = pl.BlockSpec(memory_space=pltpu.SMEM)
    dma = pltpu.SemaphoreType.DMA
    return pl.pallas_call(
        functools.partial(kernel, bricks, groups),
        out_shape=(
            jax.ShapeDtypeStruct(warm_start.shape, f32),
            jax.ShapeDtypeStruct((2, 8), f32),
            jax.ShapeDtypeStruct((2, slab, width), f32),
        ),
        in_specs=[smem] * 4 + [vmem] * 3,
        out_specs=(vmem,) * 3,
        scratch_shapes=[
            pltpu.VMEM((4, height, width), f32),
            pltpu.VMEM((2, height, width), f32),
            pltpu.VMEM((2, 3, height, width), f32),
            pltpu.VMEM((2, 3, height, width), f32),
            pltpu.VMEM((2, 5, 12, height, width), f32),
            pltpu.VMEM((3, 12, height, width), f32),
            pltpu.VMEM((2, 5, 3, height, width), f32),
            pltpu.VMEM((2, 3, 3, height, width), f32),
            pltpu.VMEM((2, groups, 9 * slab + 16, width), f32),
            pltpu.VMEM((8, 9 * slab + 16, width), f32),
            pltpu.VMEM((8, TERMS, 2, slab, width), f32),
            pltpu.VMEM((len(PAIRS), 2, slab, width), f32),
            pltpu.VMEM((64, width), f32),
            pltpu.VMEM((64, width), f32),
            pltpu.VMEM((2, bricks, 8, width), f32),
            pltpu.VMEM((groups, 8, width), f32),
            pltpu.VMEM((bricks, 8, width), f32),
            dma((2,)), dma((2,)),
            dma((2, 2)), dma((2, 2)),
            dma((2, 2)), dma((2, 2)),
            dma((2, bricks - 1)), dma((2, bricks - 1)),
            dma((2, groups - 1)), dma((2, groups - 1)),
            dma((groups - 1,)), dma((groups - 1,)),
            dma((bricks - 1,)), dma((bricks - 1,)),
        ],
        compiler_params=pltpu.CompilerParams(
            collective_id=0, has_side_effects=True, vmem_limit_bytes=40 * 2**20
        ),
    )(case_table, multiplier, target, penalty_steps, density, phase, warm_start)


def solution(mesh):
    return jax.shard_map(
        functools.partial(on_device, mesh.shape["brick"], mesh.shape["case"]),
        mesh=mesh,
        in_specs=(
            P(("parts", "brick"), None, None),
            P(("parts", "brick"), None, None),
            P(("parts", "case"), None, "brick", None, None),
            P(),
            P(),
            P(),
            P(),
        ),
        out_specs=(
            P(("parts", "case"), None, "brick", None, None),
            P(("parts", "case"), None),
            P(("parts", "brick"), "case", None),
        ),
        check_vma=False,
    )
```

```python
import functools

import jax
import jax.numpy as jnp
import numpy as np
from jax import lax
from jax.experimental import pallas as pl
from jax.experimental.pallas import tpu as pltpu
from jax.sharding import PartitionSpec as P


def element_matrix():
    ratio = 0.3
    lame = ratio / ((1.0 + ratio) * (1.0 - 2.0 * ratio))
    shear = 1.0 / (2.0 * (1.0 + ratio))
    elastic = np.zeros((6, 6))
    elastic[:3, :3] = lame
    for index in range(3):
        elastic[index, index] = lame + 2.0 * shear
        elastic[index + 3, index + 3] = shear
    points = [0.5 - 0.5 / np.sqrt(3.0), 0.5 + 0.5 / np.sqrt(3.0)]
    result = np.zeros((24, 24))
    for gx in points:
        for gy in points:
            for gz in points:
                strain_map = np.zeros((6, 24))
                for a in range(2):
                    for b in range(2):
                        for c in range(2):
                            node = 4 * a + 2 * b + c
                            fx = gx if a else 1.0 - gx
                            fy = gy if b else 1.0 - gy
                            fz = gz if c else 1.0 - gz
                            sx = 1.0 if a else -1.0
                            sy = 1.0 if b else -1.0
                            sz = 1.0 if c else -1.0
                            dxn = sx * fy * fz
                            dyn = fx * sy * fz
                            dzn = fx * fy * sz
                            strain_map[0, node] = dxn
                            strain_map[1, 8 + node] = dyn
                            strain_map[2, 16 + node] = dzn
                            strain_map[3, 8 + node] = dzn
                            strain_map[3, 16 + node] = dyn
                            strain_map[4, node] = dzn
                            strain_map[4, 16 + node] = dxn
                            strain_map[5, node] = dyn
                            strain_map[5, 8 + node] = dxn
                result = result + strain_map.T @ elastic @ strain_map / 8.0
    return result


def strain_table():
    table = np.zeros((6, 24))
    for a in range(2):
        for b in range(2):
            for c in range(2):
                node = 4 * a + 2 * b + c
                table[0, node] = a
                table[1, 8 + node] = b
                table[2, 16 + node] = c
                table[3, 8 + node] = 0.5 * c
                table[3, 16 + node] = 0.5 * b
                table[4, node] = 0.5 * c
                table[4, 16 + node] = 0.5 * a
                table[5, node] = 0.5 * b
                table[5, 8 + node] = 0.5 * a
    return table


def mode_factor():
    butterfly = np.array([[1.0, 1.0], [-1.0, 1.0]])
    modes = np.kron(np.eye(3), np.kron(butterfly, np.kron(butterfly, butterfly)))
    left = modes @ element_matrix() @ modes.T / 64.0
    rows = []
    for index in range(24):
        if left[index, index] > 1e-9:
            row = left[index] / np.sqrt(left[index, index])
            row[np.abs(row) < 1e-9] = 0.0
            rows.append(row)
            left = left - np.outer(row, row)
    factor = np.stack(rows)
    unit = strain_table() @ modes.T @ factor.T
    unit[np.abs(unit) < 1e-9] = 0.0
    rows = [[(int(i), float(row[i])) for i in np.nonzero(row)[0]] for row in factor]
    columns = [
        [(j, float(factor[j, i])) for j in range(len(rows)) if factor[j, i] != 0.0]
        for i in range(24)
    ]
    return rows, columns, unit


ROWS, COLUMNS, UNIT = mode_factor()
TERMS = len(ROWS)
PAIRS = [(i, j) for i in range(8) for j in range(i, 8)]


def total_of(terms):
    return functools.reduce(lambda x, y: x + y, terms)


def plane_modes(v):
    ahead = pltpu.roll(v, v.shape[1] - 1, 1)
    result = [None] * 4
    for c, part in enumerate((v + ahead, ahead - v)):
        up = pltpu.roll(part, v.shape[0] - 1, 0)
        result[c] = part + up
        result[2 + c] = up - part
    return result


def plane_spread(g):
    sums = [g[c] - g[2 + c] + pltpu.roll(g[c] + g[2 + c], 1, 0) for c in range(2)]
    return sums[0] - sums[1] + pltpu.roll(sums[0] + sums[1], 1, 1)


def cell_terms(lower, upper):
    modes = {}
    for comp in range(3):
        for bc in range(4):
            lo, hi = lower[comp * 4 + bc], upper[comp * 4 + bc]
            modes[comp * 8 + bc] = lo + hi
            modes[comp * 8 + 4 + bc] = hi - lo
    return [total_of([weight * modes[i] for i, weight in row]) for row in ROWS]


def cell_spread(terms):
    lower, upper = [], []
    for comp in range(3):
        for bc in range(4):
            even = COLUMNS[comp * 8 + bc]
            odd = COLUMNS[comp * 8 + 4 + bc]
            slope = total_of([weight * terms[j] for j, weight in odd])
            if even:
                mean = total_of([weight * terms[j] for j, weight in even])
                lower.append(mean - slope)
                upper.append(mean + slope)
            else:
                lower.append(-slope)
                upper.append(slope)
    return lower, upper


def unit_terms(name):
    result = {}
    for j in range(TERMS):
        picks = [
            jnp.where(name == s, float(UNIT[s, j]), 0.0) for s in range(6) if UNIT[s, j] != 0.0
        ]
        if picks:
            result[j] = total_of(picks)
    return result


def fold(x):
    return jnp.sum(x.reshape(-1, 8, x.shape[-1]), axis=0)


def kernel(
    bricks, groups, table_in, multiplier_in, target_in, steps_in, density_in, phase_in, warm_in,
    fluct, tensor, gradient,
    table, multiplier, target, steps, density, phase, warm,
    moduli, slope, below, above, modes, forces, res, image, packed, fields, terms,
    products, sums, spread, reduced, second,
    modulus_send, modulus_recv, warm_send, warm_recv, res_send, res_recv,
    red_send, red_recv, field_send, field_recv, second_send, second_recv, in_sem,
):
    brick = lax.axis_index("brick")
    group = lax.axis_index("case")
    height, width = warm.shape[3], warm.shape[4]
    slab = height // groups
    up = lax.rem(brick + 1, bricks)
    down = lax.rem(brick + bricks - 1, bricks)

    peers = [(i, j) for i in range(bricks) for j in range(groups) if (i, j) != (0, 0)]

    def place_of(step):
        return {
            "brick": lax.rem(brick + step[0], bricks), "case": lax.rem(group + step[1], groups)
        }

    loads = [
        pltpu.make_async_copy(src, dst, in_sem.at[i])
        for i, (src, dst) in enumerate([
            (density_in, density), (phase_in, phase), (warm_in, warm), (table_in, table),
            (multiplier_in, multiplier), (target_in, target), (steps_in, steps),
        ])
    ]
    for load in loads:
        load.start()
    barrier = pltpu.get_barrier_semaphore()
    for step in peers:
        pl.semaphore_signal(
            barrier, inc=1, device_id=place_of(step), device_id_type=pl.DeviceIdType.MESH
        )

    for load in loads:
        load.wait()
    kind = phase[...]
    scale = 0.5 + 0.5 * (kind >= 1).astype(jnp.float32) + 1.0 * (kind >= 2).astype(jnp.float32)
    square = density[...] * density[...]
    moduli[1:3] = 0.05 + square * density[...] * scale
    slope[...] = 3.0 * square * scale

    pl.semaphore_wait(barrier, len(peers))
    pending = []

    def send(src, dst, send_sem, recv_sem, **where):
        copy = pltpu.make_async_remote_copy(
            src_ref=src, dst_ref=dst, send_sem=send_sem, recv_sem=recv_sem,
            device_id=where, device_id_type=pl.DeviceIdType.MESH,
        )
        copy.start()
        pending.append(copy)
        return copy

    modulus_copies = [
        send(moduli.at[1], moduli.at[3], modulus_send.at[0], modulus_recv.at[0], brick=down),
        send(moduli.at[2], moduli.at[0], modulus_send.at[1], modulus_recv.at[1], brick=up),
    ]
    warm_copies = [
        [
            send(warm.at[k, :, 0], above.at[k], warm_send.at[k, 0], warm_recv.at[k, 0], brick=down),
            send(warm.at[k, :, 1], below.at[k], warm_send.at[k, 1], warm_recv.at[k, 1], brick=up),
        ]
        for k in range(2)
    ]

    def into_modes(k, node, values):
        for comp in range(3):
            for bc, part in enumerate(plane_modes(values(comp))):
                modes[k, node, comp * 4 + bc] = part

    def apply(k, first_element, count, constant):
        def chunk(index, carry):
            rows = pl.ds(pl.multiple_of(index * 8, 8), 8)
            lower = [modes[k, 0, i, rows] for i in range(12)]
            before = None
            for e in range(count):
                upper = [modes[k, e + 1, i, rows] for i in range(12)]
                found = cell_terms(lower, upper)
                if constant is not None:
                    found = [
                        constant[j] - z if j in constant else -z for j, z in enumerate(found)
                    ]
                modulus = moduli[e, rows]
                on_lower, on_upper = cell_spread([modulus * z for z in found])
                if before is not None:
                    for i in range(12):
                        forces[e - 1, i, rows] = before[i] + on_lower[i]
                before = on_upper
                lower = upper
            return carry

        lax.fori_loop(0, height // 8, chunk, 0)

    def node_force(node, comp):
        return plane_spread([forces[node, comp * 4 + bc] for bc in range(4)])

    for k in range(2):
        for node in range(2):
            into_modes(k, node + 1, lambda comp: warm[k, comp, node])
    res_copies = []
    for k in range(2):
        if k == 0:
            for copy in modulus_copies:
                copy.wait_recv()
        for copy in warm_copies[k]:
            copy.wait_recv()
        into_modes(k, 0, lambda comp: below[k, comp])
        into_modes(k, 3, lambda comp: above[k, comp])
        apply(k, 0, 3, unit_terms(table[group * 2 + k]))
        for node in range(2):
            for comp in range(3):
                res[k, node + 1, comp] = node_force(node, comp)
        res_copies.append([
            send(res.at[k, pl.ds(1, 2)], res.at[k, pl.ds(3, 2)], res_send.at[k, 0], res_recv.at[k, 0], brick=down),
            send(res.at[k, 2], res.at[k, 0], res_send.at[k, 1], res_recv.at[k, 1], brick=up),
        ])
    red_copies, field_copies = [], []

    def second_image(k):
        for node in (1, 2):
            into_modes(k, node, lambda comp: res[k, node, comp])
        for copy in res_copies[k]:
            copy.wait_recv()
        for node in (0, 3, 4):
            into_modes(k, node, lambda comp: res[k, node, comp])
        apply(k, 0, 4, None)
        squares = [jnp.zeros((8, width), jnp.float32) for _ in range(3)]
        for node in range(3):
            for comp in range(3):
                value = node_force(node, comp)
                image[k, node, comp] = value
                for bc, part in enumerate(plane_modes(value)):
                    modes[k, node, comp * 4 + bc] = part
                if node < 2:
                    own = res[k, node + 1, comp]
                    squares[0] += fold(own * own)
                    squares[1] += fold(own * value)
                    squares[2] += fold(value * value)

        def energy(index, carry):
            rows = pl.ds(pl.multiple_of(index * 8, 8), 8)
            lower = [modes[k, 0, i, rows] for i in range(12)]
            for e in range(2):
                upper = [modes[k, e + 1, i, rows] for i in range(12)]
                found = cell_terms(lower, upper)
                carry = carry + moduli[e + 1, rows] * total_of([z * z for z in found])
                lower = upper
            return carry

        squares.append(lax.fori_loop(0, height // 8, energy, jnp.zeros((8, width), jnp.float32)))
        lines = [jnp.sum(s, axis=0, keepdims=True) for s in squares]
        lines.append(jnp.zeros((4, width), jnp.float32))
        reduced[k, brick] = jnp.concatenate(lines, axis=0)
        red_copies.append([
            send(
                reduced.at[k, brick], reduced.at[k, brick], red_send.at[k, step - 1],
                red_recv.at[k, step - 1], brick=lax.rem(brick + step, bricks),
            )
            for step in range(1, bricks)
        ])
    def finish(k):
        for copy in red_copies[k]:
            copy.wait_recv()
        moments = jnp.sum(jnp.sum(reduced[k], axis=0), axis=1, keepdims=True)
        rr, rar, pp, pap = (moments[i : i + 1] for i in range(4))
        alpha = rr / rar
        later = alpha * alpha * pp - rr
        grow = 1.0 + later / rr
        curve = grow * grow * rar - 2.0 * grow * alpha * pp + alpha * alpha * pap
        alpha_later = later / curve
        on_res = alpha + alpha_later * grow
        on_image = -alpha_later * alpha
        for node in range(3):
            for comp in range(3):
                start = above[k, comp] if node == 2 else warm[k, comp, node]
                value = start + on_res * res[k, node + 1, comp] + on_image * image[k, node, comp]
                if node < 2:
                    fluct[k, comp, node] = value
                place = node * 3 + comp
                for g in range(groups):
                    packed[k, g, place * slab : (place + 1) * slab] = value[g * slab : (g + 1) * slab]
                    edge = (g + 1) * slab % height
                    packed[k, g, 9 * slab + place : 9 * slab + place + 1] = value[edge : edge + 1]
        for g in range(groups):
            packed[k, g, 9 * slab + 9 : 9 * slab + 16] = jnp.zeros((7, width), jnp.float32)
        field_copies.append([])
        for step in range(1, groups):
            peer = lax.rem(group + step, groups)
            field_copies[k].append(send(
                packed.at[k, peer], fields.at[group * 2 + k], field_send.at[k, step - 1],
                field_recv.at[k, step - 1], case=peer,
            ))
        fields[group * 2 + k] = packed[k, group]

    last = lax.broadcasted_iota(jnp.int32, (slab, width), 0) == slab - 1

    def case_terms(k, which):
        constant = unit_terms(table[which])
        lower = None
        for node in range(3):
            upper = []
            for comp in range(3):
                place = node * 3 + comp
                v = fields[which, place * slab : (place + 1) * slab]
                edge = fields[which, 9 * slab + place : 9 * slab + place + 1]
                next_v = jnp.where(last, edge, pltpu.roll(v, slab - 1, 0))
                ahead, next_ahead = pltpu.roll(v, width - 1, 1), pltpu.roll(next_v, width - 1, 1)
                s, d = v + ahead, ahead - v
                ns, nd = next_v + next_ahead, next_ahead - next_v
                upper += [s + ns, d + nd, ns - s, nd - d]
            if lower is not None:
                found = cell_terms(lower, upper)
                for j, z in enumerate(found):
                    terms[which, j, node - 1] = constant[j] - z if j in constant else -z
            lower = upper

    own_rows = pl.ds(pl.multiple_of(group * slab, slab), slab)
    own_moduli = moduli[1:3, own_rows]

    def pair_products(chosen):
        for i, j in chosen:
            value = terms[i, 0] * terms[j, 0]
            for t in range(1, TERMS):
                value = value + terms[i, t] * terms[j, t]
            products[PAIRS.index((i, j))] = value
            line = fold((value * own_moduli).reshape(2 * slab, width))
            line = jnp.sum(line, axis=0, keepdims=True)
            sums[i * 8 + j : i * 8 + j + 1] = line
            if i != j:
                sums[j * 8 + i : j * 8 + i + 1] = line

    def arrived_terms(k):
        for step in range(1, groups):
            field_copies[k][step - 1].wait_recv()
            case_terms(k, lax.rem(group + groups - step, groups) * 2 + k)

    early = [pair for pair in PAIRS if pair[0] % 2 == 0 and pair[1] % 2 == 0]
    second_image(0)
    finish(0)
    case_terms(0, group * 2)
    second_image(1)
    arrived_terms(0)
    finish(1)
    pair_products(early)
    case_terms(1, group * 2 + 1)
    arrived_terms(1)
    pair_products([pair for pair in PAIRS if pair not in early])
    totals = jnp.sum(sums[...], axis=1, keepdims=True)
    lane = lax.broadcasted_iota(jnp.int32, (8, width), 1)
    row = lax.broadcasted_iota(jnp.int32, (8, width), 0)
    tile = jnp.zeros((8, width), jnp.float32)
    for i in range(8):
        line = jnp.sum(jnp.where(lane == row, totals[i * 8 : i * 8 + 8], 0.0), axis=0, keepdims=True)
        tile = jnp.where(row == i, line, tile)
    mine = brick * groups + group
    second[mine] = tile
    copies = [
        send(second.at[mine], second.at[mine], second_send.at[i], second_recv.at[i], **place_of(step))
        for i, step in enumerate(peers)
    ]
    for copy in copies:
        copy.wait_recv()
    tile = jnp.sum(second[...], axis=0) * (1.0 / (bricks * 2 * height * width))
    for k in range(2):
        line = jnp.sum(jnp.where(row == group * 2 + k, tile, 0.0), axis=0, keepdims=True)
        tensor[k : k + 1] = line[:, :8]
    for i in range(8):
        picked = jnp.where(lane == row, jnp.broadcast_to(tile[i : i + 1], (8, width)), 0.0)
        spread[i * 8 : i * 8 + 8] = jnp.broadcast_to(jnp.sum(picked, axis=1, keepdims=True), (8, width))

    def weight(i, j):
        penalty = 0.25 * (jnp.int32(1) << steps[i, j]).astype(jnp.float32)
        return multiplier[i, j] + penalty * (spread[i * 8 + j : i * 8 + j + 1] - target[i, j])

    active = [jnp.where(table[i] < 6, 1.0, 0.0) for i in range(8)]
    result = jnp.zeros((2, slab, width), jnp.float32)
    for index, (i, j) in enumerate(PAIRS):
        both = weight(i, j) if i == j else weight(i, j) + weight(j, i)
        both = (active[i] * active[j]) * both
        result = result + both[None] * products[index]
    gradient[...] = slope[:, own_rows] * result
    for copy in pending:
        copy.wait_send()


def on_device(bricks, groups, density, phase, warm_start, case_table, multiplier, target, penalty_steps):
    height, width = density.shape[1:]
    slab = height // groups
    f32 = jnp.float32
    vmem = pl.BlockSpec(memory_space=pltpu.VMEM)
    hbm = pl.BlockSpec(memory_space=pltpu.HBM)
    dma = pltpu.SemaphoreType.DMA
    return pl.pallas_call(
        functools.partial(kernel, bricks, groups),
        out_shape=(
            jax.ShapeDtypeStruct(warm_start.shape, f32),
            jax.ShapeDtypeStruct((2, 8), f32),
            jax.ShapeDtypeStruct((2, slab, width), f32),
        ),
        in_specs=[hbm] * 7,
        out_specs=(vmem,) * 3,
        scratch_shapes=[
            pltpu.SMEM((8,), jnp.int32),
            pltpu.SMEM((8, 8), f32),
            pltpu.SMEM((8, 8), f32),
            pltpu.SMEM((8, 8), jnp.int32),
            pltpu.VMEM(density.shape, f32),
            pltpu.VMEM(phase.shape, jnp.int32),
            pltpu.VMEM(warm_start.shape, f32),
            pltpu.VMEM((4, height, width), f32),
            pltpu.VMEM((2, height, width), f32),
            pltpu.VMEM((2, 3, height, width), f32),
            pltpu.VMEM((2, 3, height, width), f32),
            pltpu.VMEM((2, 5, 12, height, width), f32),
            pltpu.VMEM((3, 12, height, width), f32),
            pltpu.VMEM((2, 5, 3, height, width), f32),
            pltpu.VMEM((2, 3, 3, height, width), f32),
            pltpu.VMEM((2, groups, 9 * slab + 16, width), f32),
            pltpu.VMEM((8, 9 * slab + 16, width), f32),
            pltpu.VMEM((8, TERMS, 2, slab, width), f32),
            pltpu.VMEM((len(PAIRS), 2, slab, width), f32),
            pltpu.VMEM((64, width), f32),
            pltpu.VMEM((64, width), f32),
            pltpu.VMEM((2, bricks, 8, width), f32),
            pltpu.VMEM((bricks * groups, 8, width), f32),
            dma((2,)), dma((2,)),
            dma((2, 2)), dma((2, 2)),
            dma((2, 2)), dma((2, 2)),
            dma((2, bricks - 1)), dma((2, bricks - 1)),
            dma((2, groups - 1)), dma((2, groups - 1)),
            dma((bricks * groups - 1,)), dma((bricks * groups - 1,)),
            dma((7,)),
        ],
        compiler_params=pltpu.CompilerParams(
            collective_id=0, has_side_effects=True, vmem_limit_bytes=40 * 2**20
        ),
    )(case_table, multiplier, target, penalty_steps, density, phase, warm_start)


def solution(mesh):
    return jax.shard_map(
        functools.partial(on_device, mesh.shape["brick"], mesh.shape["case"]),
        mesh=mesh,
        in_specs=(
            P(("parts", "brick"), None, None),
            P(("parts", "brick"), None, None),
            P(("parts", "case"), None, "brick", None, None),
            P(),
            P(),
            P(),
            P(),
        ),
        out_specs=(
            P(("parts", "case"), None, "brick", None, None),
            P(("parts", "case"), None),
            P(("parts", "brick"), "case", None),
        ),
        check_vma=False,
    )
```

```python
import functools

import jax
import jax.numpy as jnp
import numpy as np
from jax import lax
from jax.experimental import pallas as pl
from jax.experimental.pallas import tpu as pltpu
from jax.sharding import PartitionSpec as P


def element_matrix():
    ratio = 0.3
    lame = ratio / ((1.0 + ratio) * (1.0 - 2.0 * ratio))
    shear = 1.0 / (2.0 * (1.0 + ratio))
    elastic = np.zeros((6, 6))
    elastic[:3, :3] = lame
    for index in range(3):
        elastic[index, index] = lame + 2.0 * shear
        elastic[index + 3, index + 3] = shear
    points = [0.5 - 0.5 / np.sqrt(3.0), 0.5 + 0.5 / np.sqrt(3.0)]
    result = np.zeros((24, 24))
    for gx in points:
        for gy in points:
            for gz in points:
                strain_map = np.zeros((6, 24))
                for a in range(2):
                    for b in range(2):
                        for c in range(2):
                            node = 4 * a + 2 * b + c
                            fx = gx if a else 1.0 - gx
                            fy = gy if b else 1.0 - gy
                            fz = gz if c else 1.0 - gz
                            sx = 1.0 if a else -1.0
                            sy = 1.0 if b else -1.0
                            sz = 1.0 if c else -1.0
                            dxn = sx * fy * fz
                            dyn = fx * sy * fz
                            dzn = fx * fy * sz
                            strain_map[0, node] = dxn
                            strain_map[1, 8 + node] = dyn
                            strain_map[2, 16 + node] = dzn
                            strain_map[3, 8 + node] = dzn
                            strain_map[3, 16 + node] = dyn
                            strain_map[4, node] = dzn
                            strain_map[4, 16 + node] = dxn
                            strain_map[5, node] = dyn
                            strain_map[5, 8 + node] = dxn
                result = result + strain_map.T @ elastic @ strain_map / 8.0
    return result


def strain_table():
    table = np.zeros((6, 24))
    for a in range(2):
        for b in range(2):
            for c in range(2):
                node = 4 * a + 2 * b + c
                table[0, node] = a
                table[1, 8 + node] = b
                table[2, 16 + node] = c
                table[3, 8 + node] = 0.5 * c
                table[3, 16 + node] = 0.5 * b
                table[4, node] = 0.5 * c
                table[4, 16 + node] = 0.5 * a
                table[5, node] = 0.5 * b
                table[5, 8 + node] = 0.5 * a
    return table


def mode_factor():
    butterfly = np.array([[1.0, 1.0], [-1.0, 1.0]])
    modes = np.kron(np.eye(3), np.kron(butterfly, np.kron(butterfly, butterfly)))
    left = modes @ element_matrix() @ modes.T / 64.0
    rows = []
    for index in range(24):
        if left[index, index] > 1e-9:
            row = left[index] / np.sqrt(left[index, index])
            row[np.abs(row) < 1e-9] = 0.0
            rows.append(row)
            left = left - np.outer(row, row)
    factor = np.stack(rows)
    unit = strain_table() @ modes.T @ factor.T
    unit[np.abs(unit) < 1e-9] = 0.0
    rows = [[(int(i), float(row[i])) for i in np.nonzero(row)[0]] for row in factor]
    columns = [
        [(j, float(factor[j, i])) for j in range(len(rows)) if factor[j, i] != 0.0]
        for i in range(24)
    ]
    return rows, columns, unit


ROWS, COLUMNS, UNIT = mode_factor()
TERMS = len(ROWS)
PAIRS = [(i, j) for i in range(8) for j in range(i, 8)]


def total_of(terms):
    return functools.reduce(lambda x, y: x + y, terms)


def plane_modes(v):
    ahead = pltpu.roll(v, v.shape[1] - 1, 1)
    result = [None] * 4
    for c, part in enumerate((v + ahead, ahead - v)):
        up = pltpu.roll(part, v.shape[0] - 1, 0)
        result[c] = part + up
        result[2 + c] = up - part
    return result


def plane_spread(g):
    sums = [g[c] - g[2 + c] + pltpu.roll(g[c] + g[2 + c], 1, 0) for c in range(2)]
    return sums[0] - sums[1] + pltpu.roll(sums[0] + sums[1], 1, 1)


def cell_terms(lower, upper):
    modes = {}
    for comp in range(3):
        for bc in range(4):
            lo, hi = lower[comp * 4 + bc], upper[comp * 4 + bc]
            modes[comp * 8 + bc] = lo + hi
            modes[comp * 8 + 4 + bc] = hi - lo
    return [total_of([weight * modes[i] for i, weight in row]) for row in ROWS]


def cell_spread(terms):
    lower, upper = [], []
    for comp in range(3):
        for bc in range(4):
            even = COLUMNS[comp * 8 + bc]
            odd = COLUMNS[comp * 8 + 4 + bc]
            slope = total_of([weight * terms[j] for j, weight in odd])
            if even:
                mean = total_of([weight * terms[j] for j, weight in even])
                lower.append(mean - slope)
                upper.append(mean + slope)
            else:
                lower.append(-slope)
                upper.append(slope)
    return lower, upper


def unit_terms(name):
    result = {}
    for j in range(TERMS):
        picks = [
            jnp.where(name == s, float(UNIT[s, j]), 0.0) for s in range(6) if UNIT[s, j] != 0.0
        ]
        if picks:
            result[j] = total_of(picks)
    return result


def fold(x):
    return jnp.sum(x.reshape(-1, 8, x.shape[-1]), axis=0)


def kernel(
    bricks, groups, table_in, multiplier_in, target_in, steps_in, density_in, phase_in, warm_in,
    fluct, tensor, gradient,
    table, multiplier, target, steps, density, phase, warm,
    moduli, slope, below, above, modes, forces, res, image, packed, fields, terms,
    products, sums, spread, reduced, second,
    modulus_send, modulus_recv, warm_send, warm_recv, res_send, res_recv,
    red_send, red_recv, field_send, field_recv, second_send, second_recv, in_sem,
):
    brick = lax.axis_index("brick")
    group = lax.axis_index("case")
    height, width = warm.shape[3], warm.shape[4]
    slab = height // groups
    up = lax.rem(brick + 1, bricks)
    down = lax.rem(brick + bricks - 1, bricks)

    peers = [(i, j) for i in range(bricks) for j in range(groups) if (i, j) != (0, 0)]

    def place_of(step):
        return {
            "brick": lax.rem(brick + step[0], bricks), "case": lax.rem(group + step[1], groups)
        }

    loads = [
        pltpu.make_async_copy(src, dst, in_sem.at[i])
        for i, (src, dst) in enumerate([
            (density_in, density), (phase_in, phase), (warm_in, warm), (table_in, table),
            (multiplier_in, multiplier), (target_in, target), (steps_in, steps),
        ])
    ]
    for load in loads:
        load.start()
    barrier = pltpu.get_barrier_semaphore()
    for step in peers:
        pl.semaphore_signal(
            barrier, inc=1, device_id=place_of(step), device_id_type=pl.DeviceIdType.MESH
        )

    for load in loads:
        load.wait()
    kind = phase[...]
    scale = 0.5 + 0.5 * (kind >= 1).astype(jnp.float32) + 1.0 * (kind >= 2).astype(jnp.float32)
    square = density[...] * density[...]
    moduli[1:3] = 0.05 + square * density[...] * scale
    slope[...] = 3.0 * square * scale

    pl.semaphore_wait(barrier, len(peers))
    pending = []

    def send(src, dst, send_sem, recv_sem, **where):
        copy = pltpu.make_async_remote_copy(
            src_ref=src, dst_ref=dst, send_sem=send_sem, recv_sem=recv_sem,
            device_id=where, device_id_type=pl.DeviceIdType.MESH,
        )
        copy.start()
        pending.append(copy)
        return copy

    modulus_copies = [
        send(moduli.at[1], moduli.at[3], modulus_send.at[0], modulus_recv.at[0], brick=down),
        send(moduli.at[2], moduli.at[0], modulus_send.at[1], modulus_recv.at[1], brick=up),
    ]
    warm_copies = [
        [
            send(warm.at[k, :, 0], above.at[k], warm_send.at[k, 0], warm_recv.at[k, 0], brick=down),
            send(warm.at[k, :, 1], below.at[k], warm_send.at[k, 1], warm_recv.at[k, 1], brick=up),
        ]
        for k in range(2)
    ]

    def into_modes(k, node, values):
        for comp in range(3):
            for bc, part in enumerate(plane_modes(values(comp))):
                modes[k, node, comp * 4 + bc] = part

    def apply(k, first_element, count, constant):
        def chunk(index, carry):
            rows = pl.ds(pl.multiple_of(index * 8, 8), 8)
            lower = [modes[k, 0, i, rows] for i in range(12)]
            before = None
            for e in range(count):
                upper = [modes[k, e + 1, i, rows] for i in range(12)]
                found = cell_terms(lower, upper)
                if constant is not None:
                    found = [
                        constant[j] - z if j in constant else -z for j, z in enumerate(found)
                    ]
                modulus = moduli[e, rows]
                on_lower, on_upper = cell_spread([modulus * z for z in found])
                if before is not None:
                    for i in range(12):
                        forces[e - 1, i, rows] = before[i] + on_lower[i]
                before = on_upper
                lower = upper
            return carry

        lax.fori_loop(0, height // 8, chunk, 0)

    def node_force(node, comp):
        return plane_spread([forces[node, comp * 4 + bc] for bc in range(4)])

    for k in range(2):
        for node in range(2):
            into_modes(k, node + 1, lambda comp: warm[k, comp, node])
    res_copies = []
    for k in range(2):
        if k == 0:
            for copy in modulus_copies:
                copy.wait_recv()
        for copy in warm_copies[k]:
            copy.wait_recv()
        into_modes(k, 0, lambda comp: below[k, comp])
        into_modes(k, 3, lambda comp: above[k, comp])
        apply(k, 0, 3, unit_terms(table[group * 2 + k]))
        for node in range(2):
            for comp in range(3):
                res[k, node + 1, comp] = node_force(node, comp)
        res_copies.append([
            send(res.at[k, pl.ds(1, 2)], res.at[k, pl.ds(3, 2)], res_send.at[k, 0], res_recv.at[k, 0], brick=down),
            send(res.at[k, 2], res.at[k, 0], res_send.at[k, 1], res_recv.at[k, 1], brick=up),
        ])
    red_copies, field_copies = [], []

    def second_image(k):
        for node in (1, 2):
            into_modes(k, node, lambda comp: res[k, node, comp])
        for copy in res_copies[k]:
            copy.wait_recv()
        for node in (0, 3, 4):
            into_modes(k, node, lambda comp: res[k, node, comp])
        apply(k, 0, 4, None)
        squares = [jnp.zeros((8, width), jnp.float32) for _ in range(3)]
        for node in range(3):
            for comp in range(3):
                value = node_force(node, comp)
                image[k, node, comp] = value
                for bc, part in enumerate(plane_modes(value)):
                    modes[k, node, comp * 4 + bc] = part
                if node < 2:
                    own = res[k, node + 1, comp]
                    squares[0] += fold(own * own)
                    squares[1] += fold(own * value)
                    squares[2] += fold(value * value)

        def energy(index, carry):
            rows = pl.ds(pl.multiple_of(index * 8, 8), 8)
            lower = [modes[k, 0, i, rows] for i in range(12)]
            for e in range(2):
                upper = [modes[k, e + 1, i, rows] for i in range(12)]
                found = cell_terms(lower, upper)
                carry = carry + moduli[e + 1, rows] * total_of([z * z for z in found])
                lower = upper
            return carry

        squares.append(lax.fori_loop(0, height // 8, energy, jnp.zeros((8, width), jnp.float32)))
        lines = [jnp.sum(s, axis=0, keepdims=True) for s in squares]
        lines.append(jnp.zeros((4, width), jnp.float32))
        reduced[k, brick] = jnp.concatenate(lines, axis=0)
        red_copies.append([
            send(
                reduced.at[k, brick], reduced.at[k, brick], red_send.at[k, step - 1],
                red_recv.at[k, step - 1], brick=lax.rem(brick + step, bricks),
            )
            for step in range(1, bricks)
        ])
    def finish(k):
        for copy in red_copies[k]:
            copy.wait_recv()
        moments = jnp.sum(jnp.sum(reduced[k], axis=0), axis=1, keepdims=True)
        rr, rar, pp, pap = (moments[i : i + 1] for i in range(4))
        alpha = rr / rar
        later = alpha * alpha * pp - rr
        grow = 1.0 + later / rr
        curve = grow * grow * rar - 2.0 * grow * alpha * pp + alpha * alpha * pap
        alpha_later = later / curve
        on_res = alpha + alpha_later * grow
        on_image = -alpha_later * alpha
        for node in range(3):
            for comp in range(3):
                start = above[k, comp] if node == 2 else warm[k, comp, node]
                value = start + on_res * res[k, node + 1, comp] + on_image * image[k, node, comp]
                if node < 2:
                    fluct[k, comp, node] = value
                place = node * 3 + comp
                for g in range(groups):
                    packed[k, g, place * slab : (place + 1) * slab] = value[g * slab : (g + 1) * slab]
                    edge = (g + 1) * slab % height
                    packed[k, g, 9 * slab + place : 9 * slab + place + 1] = value[edge : edge + 1]
        for g in range(groups):
            packed[k, g, 9 * slab + 9 : 9 * slab + 16] = jnp.zeros((7, width), jnp.float32)
        field_copies.append([])
        for step in range(1, groups):
            peer = lax.rem(group + step, groups)
            field_copies[k].append(send(
                packed.at[k, peer], fields.at[group * 2 + k], field_send.at[k, step - 1],
                field_recv.at[k, step - 1], case=peer,
            ))
        fields[group * 2 + k] = packed[k, group]

    last = lax.broadcasted_iota(jnp.int32, (slab, width), 0) == slab - 1

    def case_terms(k, which):
        constant = unit_terms(table[which])
        lower = None
        for node in range(3):
            upper = []
            for comp in range(3):
                place = node * 3 + comp
                v = fields[which, place * slab : (place + 1) * slab]
                edge = fields[which, 9 * slab + place : 9 * slab + place + 1]
                next_v = jnp.where(last, edge, pltpu.roll(v, slab - 1, 0))
                ahead, next_ahead = pltpu.roll(v, width - 1, 1), pltpu.roll(next_v, width - 1, 1)
                s, d = v + ahead, ahead - v
                ns, nd = next_v + next_ahead, next_ahead - next_v
                upper += [s + ns, d + nd, ns - s, nd - d]
            if lower is not None:
                found = cell_terms(lower, upper)
                for j, z in enumerate(found):
                    terms[which, j, node - 1] = constant[j] - z if j in constant else -z
            lower = upper

    own_rows = pl.ds(pl.multiple_of(group * slab, slab), slab)
    own_moduli = moduli[1:3, own_rows]

    def pair_products(chosen):
        for i, j in chosen:
            value = terms[i, 0] * terms[j, 0]
            for t in range(1, TERMS):
                value = value + terms[i, t] * terms[j, t]
            products[PAIRS.index((i, j))] = value
            line = fold((value * own_moduli).reshape(2 * slab, width))
            line = jnp.sum(line, axis=0, keepdims=True)
            sums[i * 8 + j : i * 8 + j + 1] = line
            if i != j:
                sums[j * 8 + i : j * 8 + i + 1] = line

    def arrived_terms(k):
        for step in range(1, groups):
            field_copies[k][step - 1].wait_recv()
            case_terms(k, lax.rem(group + groups - step, groups) * 2 + k)

    early = [pair for pair in PAIRS if pair[0] % 2 == 0 and pair[1] % 2 == 0]
    second_image(0)
    finish(0)
    case_terms(0, group * 2)
    second_image(1)
    arrived_terms(0)
    finish(1)
    pair_products(early)
    case_terms(1, group * 2 + 1)
    arrived_terms(1)
    pair_products([pair for pair in PAIRS if pair not in early])
    totals = jnp.sum(sums[...], axis=1, keepdims=True)
    lane = lax.broadcasted_iota(jnp.int32, (8, width), 1)
    row = lax.broadcasted_iota(jnp.int32, (8, width), 0)
    tile = jnp.zeros((8, width), jnp.float32)
    for i in range(8):
        line = jnp.sum(jnp.where(lane == row, totals[i * 8 : i * 8 + 8], 0.0), axis=0, keepdims=True)
        tile = jnp.where(row == i, line, tile)
    mine = brick * groups + group
    second[mine] = tile
    copies = [
        send(second.at[mine], second.at[mine], second_send.at[i], second_recv.at[i], **place_of(step))
        for i, step in enumerate(peers)
    ]
    for copy in copies:
        copy.wait_recv()
    tile = jnp.sum(second[...], axis=0) * (1.0 / (bricks * 2 * height * width))
    for k in range(2):
        line = jnp.sum(jnp.where(row == group * 2 + k, tile, 0.0), axis=0, keepdims=True)
        tensor[k : k + 1] = line[:, :8]
    for i in range(8):
        picked = jnp.where(lane == row, jnp.broadcast_to(tile[i : i + 1], (8, width)), 0.0)
        spread[i * 8 : i * 8 + 8] = jnp.broadcast_to(jnp.sum(picked, axis=1, keepdims=True), (8, width))

    def weight(i, j):
        penalty = 0.25 * (jnp.int32(1) << steps[i, j]).astype(jnp.float32)
        return multiplier[i, j] + penalty * (spread[i * 8 + j : i * 8 + j + 1] - target[i, j])

    active = [jnp.where(table[i] < 6, 1.0, 0.0) for i in range(8)]
    result = jnp.zeros((2, slab, width), jnp.float32)
    for index, (i, j) in enumerate(PAIRS):
        both = weight(i, j) if i == j else weight(i, j) + weight(j, i)
        both = (active[i] * active[j]) * both
        result = result + both[None] * products[index]
    gradient[...] = slope[:, own_rows] * result
    for copy in pending:
        copy.wait_send()


def on_device(bricks, groups, density, phase, warm_start, case_table, multiplier, target, penalty_steps):
    height, width = density.shape[1:]
    slab = height // groups
    f32 = jnp.float32
    vmem = pl.BlockSpec(memory_space=pltpu.VMEM)
    hbm = pl.BlockSpec(memory_space=pltpu.HBM)
    dma = pltpu.SemaphoreType.DMA
    return pl.pallas_call(
        functools.partial(kernel, bricks, groups),
        out_shape=(
            jax.ShapeDtypeStruct(warm_start.shape, f32),
            jax.ShapeDtypeStruct((2, 8), f32),
            jax.ShapeDtypeStruct((2, slab, width), f32),
        ),
        in_specs=[hbm] * 7,
        out_specs=(vmem,) * 3,
        scratch_shapes=[
            pltpu.SMEM((8,), jnp.int32),
            pltpu.SMEM((8, 8), f32),
            pltpu.SMEM((8, 8), f32),
            pltpu.SMEM((8, 8), jnp.int32),
            pltpu.VMEM(density.shape, f32),
            pltpu.VMEM(phase.shape, jnp.int32),
            pltpu.VMEM(warm_start.shape, f32),
            pltpu.VMEM((4, height, width), f32),
            pltpu.VMEM((2, height, width), f32),
            pltpu.VMEM((2, 3, height, width), f32),
            pltpu.VMEM((2, 3, height, width), f32),
            pltpu.VMEM((2, 5, 12, height, width), f32),
            pltpu.VMEM((3, 12, height, width), f32),
            pltpu.VMEM((2, 5, 3, height, width), f32),
            pltpu.VMEM((2, 3, 3, height, width), f32),
            pltpu.VMEM((2, groups, 9 * slab + 16, width), f32),
            pltpu.VMEM((8, 9 * slab + 16, width), f32),
            pltpu.VMEM((8, TERMS, 2, slab, width), f32),
            pltpu.VMEM((len(PAIRS), 2, slab, width), f32),
            pltpu.VMEM((64, width), f32),
            pltpu.VMEM((64, width), f32),
            pltpu.VMEM((2, bricks, 8, width), f32),
            pltpu.VMEM((bricks * groups, 8, width), f32),
            dma((2,)), dma((2,)),
            dma((2, 2)), dma((2, 2)),
            dma((2, 2)), dma((2, 2)),
            dma((2, bricks - 1)), dma((2, bricks - 1)),
            dma((2, groups - 1)), dma((2, groups - 1)),
            dma((bricks * groups - 1,)), dma((bricks * groups - 1,)),
            dma((7,)),
        ],
        compiler_params=pltpu.CompilerParams(
            collective_id=0, has_side_effects=True, vmem_limit_bytes=63 * 2**20 + 2**19
        ),
    )(case_table, multiplier, target, penalty_steps, density, phase, warm_start)


def solution(mesh):
    return jax.shard_map(
        functools.partial(on_device, mesh.shape["brick"], mesh.shape["case"]),
        mesh=mesh,
        in_specs=(
            P(("parts", "brick"), None, None),
            P(("parts", "brick"), None, None),
            P(("parts", "case"), None, "brick", None, None),
            P(),
            P(),
            P(),
            P(),
        ),
        out_specs=(
            P(("parts", "case"), None, "brick", None, None),
            P(("parts", "case"), None),
            P(("parts", "brick"), "case", None),
        ),
        check_vma=False,
    )
```
